32 devices in a mesh: dp: 8 (over z, x), tensor: 4 (over y, core).
Axes of the slice: x: 2, y: 2, z: 4, core: 2. Of those that a mesh axis runs over, the one named last changes fastest.
Arguments:
- hidden: bfloat16 [1024, 4096], P('dp', 'tensor'), may hold values from -6 to 6
- grad_out: bfloat16 [1024, 4096], P('dp', 'tensor'), may hold values from -0.59765625 to 0.59765625
- query_weight: bfloat16 [4096, 4096], P(None, 'tensor'), may hold values from -0.09375 to 0.09375
- key_weight: bfloat16 [768, 4096], P(None, 'tensor'), may hold values from -0.21875 to 0.21875
- value_weight: bfloat16 [768, 4096], P(None, 'tensor'), may hold values from -0.21875 to 0.21875
- out_weight: bfloat16 [4096, 4096], P('tensor', 'dp'), may hold values from -0.75 to 0.75
- neighbour_states: bfloat16 [32, 128, 768], P('dp', None, 'tensor'), may hold values from -6 to 6
- block_owner: int32 [8, 4], P('dp'), may hold values from 0 to 7, as said below
- slot_target: int32 [8, 4], P('dp'), may hold values from 0 to 7, as said below
Outputs:
- cross_out: bfloat16 [1024, 4096], P('dp', 'tensor')
- grad_hidden: bfloat16 [1024, 4096], P('dp', 'tensor')
- grad_states: bfloat16 [32, 128, 768], P('dp', None, 'tensor')
The draws below stay inside these ranges and needn't reach their ends.
Inputs may be any that keep to these rules, and one draw needn't show every extreme that they name: block_owner[d, t] = o exactly when slot_target[o, t] = d. The blocks 2k and 2k+1 of a dp index share their holder; the difference (holder - d) modulo the dp count is the same for every d, lies in 1 to 4, and differs between k. So a dp index holds exactly 2 blocks for each of 2 other indices. `slot_target`: the inverse map of block_owner, as stated there.
All inputs are finite; a program needn't handle non-finite values.
Results may differ from the reference program's by a relative error of at most 0.012.
Values may be sent and summed in bfloat16 or wider, within the bound.
A program may use at most 128 MiB of HBM per device.

```python
import math
import jax
import jax.numpy as jnp
from jax import lax

D = 4096
HEADS = 32
HD = 128
DE = 768
SPAN = 64
NBR = 128
K_NB = 2
CH_DEV = 2
WINDOW = 4
NEED = 4
TOKENS = 1024
BLOCKS = 32
N_DP = 8
N_TENSOR = 4


def owner_offsets(key):
    shuffled = jax.random.permutation(jax.random.fold_in(key, 11), WINDOW)
    return jnp.repeat(shuffled[:CH_DEV] + 1, K_NB).astype(jnp.int32)


def draw_block_owner(key, part):
    offsets = owner_offsets(key)
    device_ids = jnp.arange(N_DP, dtype=jnp.int32)[:, None]
    return ((device_ids + offsets[None, :]) % N_DP).astype(jnp.int32)


def draw_slot_target(key, part):
    offsets = owner_offsets(key)
    device_ids = jnp.arange(N_DP, dtype=jnp.int32)[:, None]
    return ((device_ids - offsets[None, :] + N_DP) % N_DP).astype(jnp.int32)


def shard_levels(stream_key, dims, pieces, smallest, largest):
    factor_of, own = 1.0, jax.random.fold_in(stream_key, 6)
    for position, parts in pieces:
        heights = jnp.exp(jax.random.uniform(jax.random.fold_in(own, position), (parts,), jnp.float32, smallest / len(pieces), largest / len(pieces)))
        factor_of = factor_of * jnp.repeat(heights, dims[position] // parts).reshape([-1 if axis == position else 1 for axis in range(len(dims))])
    return factor_of


def bell_draw(stream_key, dims, spread, bound, shards=(), kind=jnp.bfloat16):
    array = spread * jax.random.normal(stream_key, dims, jnp.float32)
    if shards:
        array = array * shard_levels(stream_key, dims, shards, -0.22, 0.18)
    return jnp.clip(array, -bound, bound).astype(kind)


def setup_inputs(seed: int = 0) -> dict:
    key_list = jax.random.split(jax.random.key(seed), 10)
    hidden = bell_draw(key_list[0], (TOKENS, D), 1.0, 6.0, ((0, 8), (1, 4)))
    grad_out = bell_draw(key_list[1], (TOKENS, D), 0.1, 0.59765625, ((0, 8), (1, 4)))
    query_weight = bell_draw(key_list[2], (D, D), D ** -0.5, 0.09375, ((1, 4),))
    key_weight = bell_draw(key_list[3], (DE, D), DE ** -0.5, 0.21875, ((1, 4),))
    value_weight = bell_draw(key_list[4], (DE, D), DE ** -0.5, 0.21875, ((1, 4),))
    out_weight = bell_draw(key_list[5], (D, D), 64 ** -0.5, 0.75, ((0, 4), (1, 8)))
    neighbour_states = bell_draw(key_list[6], (BLOCKS, NBR, DE), 1.0, 6.0, ((0, 8), (2, 4)))
    block_owner = draw_block_owner(jax.random.fold_in(key_list[9], 71), 0)
    slot_target = draw_slot_target(jax.random.fold_in(key_list[9], 71), 0)
    return {"hidden": hidden, "grad_out": grad_out, "query_weight": query_weight, "key_weight": key_weight, "value_weight": value_weight, "out_weight": out_weight, "neighbour_states": neighbour_states, "block_owner": block_owner, "slot_target": slot_target}


def grouped_sum(left, right_t, groups):
    width = left.shape[1] // groups
    total = jnp.zeros((left.shape[0], right_t.shape[1]), jnp.float32)
    for group in range(groups):
        piece = jnp.dot(left[:, group * width:(group + 1) * width], right_t[group * width:(group + 1) * width, :], preferred_element_type=jnp.float32)
        total = total + piece.astype(jnp.bfloat16).astype(jnp.float32)
    return total

def reference(hidden, grad_out, query_weight, key_weight, value_weight, out_weight, neighbour_states, block_owner, slot_target):
    block_ids = jnp.arange(NEED, dtype=jnp.int32)
    rows_in = (block_owner * NEED + block_ids[None, :]).reshape(-1).astype(jnp.int32)
    neighbours = jnp.take(neighbour_states, rows_in, axis=0)
    span_count = TOKENS // SPAN
    score_scale = 1.0 / math.sqrt(HD)
    query = jnp.dot(hidden, query_weight, preferred_element_type=jnp.float32).astype(jnp.bfloat16)
    flat_states = neighbours.reshape(-1, DE)
    key = jnp.dot(flat_states, key_weight, preferred_element_type=jnp.float32).astype(jnp.bfloat16)
    value = jnp.dot(flat_states, value_weight, preferred_element_type=jnp.float32).astype(jnp.bfloat16)
    query_heads = query.astype(jnp.float32).reshape(span_count, SPAN, HEADS, HD)
    key_heads = key.astype(jnp.float32).reshape(span_count, K_NB * NBR, HEADS, HD)
    value_heads = value.astype(jnp.float32).reshape(span_count, K_NB * NBR, HEADS, HD)
    scores = jnp.einsum('cqhd,ckhd->chqk', query_heads, key_heads) * score_scale
    highest = lax.optimization_barrier(jnp.max(scores, axis=-1, keepdims=True))
    expanded = jnp.exp(scores - highest)
    probs = expanded / lax.optimization_barrier(jnp.sum(expanded, axis=-1, keepdims=True))
    probs_low = probs.astype(jnp.bfloat16)
    attended = jnp.einsum('chqk,ckhd->cqhd', probs_low.astype(jnp.float32), value_heads).astype(jnp.bfloat16).reshape(TOKENS, D)
    cross_out = grouped_sum(attended, out_weight, N_TENSOR).astype(jnp.bfloat16)
    grad_attended = jnp.dot(grad_out, out_weight.T, preferred_element_type=jnp.float32).astype(jnp.bfloat16)
    grad_heads = grad_attended.astype(jnp.float32).reshape(span_count, SPAN, HEADS, HD)
    grad_probs = jnp.einsum('cqhd,ckhd->chqk', grad_heads, value_heads)
    grad_scores = (probs * (grad_probs - lax.optimization_barrier(jnp.sum(probs * grad_probs, axis=-1, keepdims=True))) * score_scale).astype(jnp.bfloat16)
    grad_scores_f = grad_scores.astype(jnp.float32)
    grad_query = jnp.einsum('chqk,ckhd->cqhd', grad_scores_f, key_heads).astype(jnp.bfloat16).reshape(TOKENS, D)
    grad_key = jnp.einsum('chqk,cqhd->ckhd', grad_scores_f, query_heads).astype(jnp.bfloat16).reshape(-1, D)
    grad_value = jnp.einsum('chqk,cqhd->ckhd', probs_low.astype(jnp.float32), grad_heads).astype(jnp.bfloat16).reshape(-1, D)
    grad_hidden = grouped_sum(grad_query, query_weight.T, N_TENSOR).astype(jnp.bfloat16)
    width = D // N_TENSOR
    states_total = jnp.zeros((grad_key.shape[0], DE), jnp.float32)
    for group in range(N_TENSOR):
        lower = group * width
        upper = lower + width
        piece = jnp.dot(grad_key[:, lower:upper], key_weight[:, lower:upper].T, preferred_element_type=jnp.float32) + jnp.dot(grad_value[:, lower:upper], value_weight[:, lower:upper].T, preferred_element_type=jnp.float32)
        states_total = states_total + piece.astype(jnp.bfloat16).astype(jnp.float32)
    grad_neighbours = states_total.astype(jnp.bfloat16).reshape(BLOCKS, NBR, DE)
    rows_out = (slot_target * NEED + block_ids[None, :]).reshape(-1).astype(jnp.int32)
    grad_states = jnp.take(grad_neighbours, rows_out, axis=0)
    return (cross_out, grad_hidden, grad_states)
```

```python
import functools
import math

import jax
import jax.numpy as jnp
from jax import lax
from jax.experimental import pallas as pl
from jax.experimental.pallas import tpu as pltpu
from jax.sharding import PartitionSpec as P

HEADS = 32
SPAN = 64
K_NB = 2
CAP = 2
WINDOW = 4
BF = jnp.bfloat16
F32 = jnp.float32


def dot_nt(left, right):
    return lax.dot_general(left, right, (((1,), (1,)), ((), ())), preferred_element_type=F32)


def dot_tn(left, right):
    return lax.dot_general(left, right, (((0,), (0,)), ((), ())), preferred_element_type=F32)


def dot(left, right):
    return jnp.dot(left, right, preferred_element_type=F32)


def softmax_rows(q, k, scale):
    scores = dot_nt(q, k) * scale
    expanded = jnp.exp(scores - jnp.max(scores, axis=-1, keepdims=True))
    return expanded / jnp.sum(expanded, axis=-1, keepdims=True)


def forward_kernel(spans, keys, scale, q_ref, k_ref, v_ref, att_ref):
    for c in range(spans):
        rows, cols = pl.ds(c * SPAN, SPAN), pl.ds(c * keys, keys)
        probs = softmax_rows(q_ref[rows, :], k_ref[cols, :], scale)
        att_ref[rows, :] = dot(probs.astype(BF), v_ref[cols, :]).astype(BF)


def backward_kernel(spans, keys, scale, q_ref, k_ref, v_ref, ga_ref, gq_ref, gk_ref, gv_ref):
    for c in range(spans):
        rows, cols = pl.ds(c * SPAN, SPAN), pl.ds(c * keys, keys)
        q, k, v, ga = q_ref[rows, :], k_ref[cols, :], v_ref[cols, :], ga_ref[rows, :]
        probs = softmax_rows(q, k, scale)
        gp = dot_nt(ga, v)
        gs = (probs * (gp - jnp.sum(probs * gp, axis=-1, keepdims=True)) * scale).astype(BF)
        gq_ref[rows, :] = dot(gs, k).astype(BF)
        gk_ref[cols, :] = dot_tn(gs, q).astype(BF)
        gv_ref[cols, :] = dot_tn(probs.astype(BF), ga).astype(BF)


def per_head(kernel, head_size, arrays, outs):
    heads = arrays[0].shape[1] // head_size

    def block(rows):
        return pl.BlockSpec((rows, head_size), lambda h: (0, h))

    flops = 2 * 6 * arrays[0].shape[0] * 256 * arrays[0].shape[1]
    return pl.pallas_call(
        kernel,
        grid=(heads,),
        in_specs=[block(a.shape[0]) for a in arrays],
        out_specs=[block(a.shape[0]) for a in outs],
        out_shape=[jax.ShapeDtypeStruct(a.shape, BF) for a in outs],
        cost_estimate=pl.CostEstimate(
            flops=flops, bytes_accessed=2 * sum(a.size for a in arrays + outs), transcendentals=0
        ),
        compiler_params=pltpu.CompilerParams(vmem_limit_bytes=32 * 2**20),
    )(*arrays)


def shards(
    hidden,
    grad_out,
    query_weight,
    key_weight,
    value_weight,
    out_weight,
    neighbour_states,
    block_owner,
    slot_target,
):
    dp_count, tp = lax.axis_size("dp"), lax.axis_size("tensor")
    g = dp_count // tp
    d, t = lax.axis_index("dp"), lax.axis_index("tensor")
    zz, gx = d // g, d % g
    tokens, width = hidden.shape
    block_count, block_len, width_part = neighbour_states.shape

    def over_tensor(x, k):
        return lax.ppermute(x, "tensor", [(i, i ^ k) for i in range(tp)])

    def over_zz(x, j):
        return lax.ppermute(x, "dp", [(i, (i // g ^ j) * g + i % g) for i in range(dp_count)])

    def transposed(x):
        pairs = [
            (((a * g + b) * tp + c), ((c * g + b) * tp + a))
            for a in range(tp)
            for b in range(g)
            for c in range(tp)
        ]
        return lax.ppermute(x, ("dp", "tensor"), pairs)

    owner_gap = (block_owner[0] - d + dp_count) % dp_count
    target_gap = (d - slot_target[0] + dp_count) % dp_count
    low, high = neighbour_states[:CAP], neighbour_states[CAP:]
    arrived = []
    for offset in range(1, WINDOW + 1):
        outgoing = jnp.where(target_gap[CAP] == offset, high, low)
        arrived.append(
            lax.ppermute(
                outgoing, "dp", [(i, (i - offset) % dp_count) for i in range(dp_count)]
            )
        )

    turned = transposed(grad_out)
    hidden_parts = [hidden] + [over_tensor(hidden, k) for k in range(1, tp)]
    weight = jnp.zeros((out_weight.shape[0], out_weight.shape[1] * g), BF)
    for k in range(g):
        part = out_weight
        if k:
            part = lax.ppermute(
                part, "dp", [(i, i // g * g + (i - k) % g) for i in range(dp_count)]
            )
        weight = lax.dynamic_update_slice(weight, part, (0, (gx + k) % g * out_weight.shape[1]))

    halves = []
    for k in range(block_count // CAP):
        picked = arrived[0]
        for offset in range(2, WINDOW + 1):
            picked = jnp.where(owner_gap[k * CAP] == offset, arrived[offset - 1], picked)
        halves.append(picked)
    delivered = jnp.concatenate(halves, axis=0).reshape(block_count * block_len, width_part)

    neighbours = jnp.zeros((tp, block_count * block_len, width_part), BF)
    for k in range(tp):
        part = over_tensor(delivered, k) if k else delivered
        neighbours = lax.dynamic_update_slice(neighbours, part[None], (t ^ k, 0, 0))
    neighbours = jnp.concatenate([neighbours[k] for k in range(tp)], axis=1)

    turned_all = jnp.concatenate(
        [turned] + [over_tensor(turned, k) for k in range(1, tp)], axis=0
    )
    partial = dot_nt(turned_all, weight).astype(BF).reshape(tp, tokens, -1)

    def piece(stack, index):
        return lax.dynamic_index_in_dim(stack, index, 0, keepdims=False)

    grad_attended = piece(partial, t ^ zz).astype(F32)
    for j in range(1, tp):
        grad_attended += over_zz(piece(partial, t ^ zz ^ j), j).astype(F32)
    grad_attended = grad_attended.astype(BF)

    query = jnp.zeros((tokens, query_weight.shape[1]), F32)
    for k in range(tp):
        rows = lax.dynamic_slice_in_dim(query_weight, (t ^ k) * width, width, 0)
        query += dot(hidden_parts[k], rows)
    query = query.astype(BF)
    key = dot(neighbours, key_weight).astype(BF)
    value = dot(neighbours, value_weight).astype(BF)

    head_size = query.shape[1] * tp // HEADS
    spans = tokens // SPAN
    scale = 1.0 / math.sqrt(head_size)
    keys = K_NB * block_len
    (attended,) = per_head(
        functools.partial(forward_kernel, spans, keys, scale),
        head_size,
        [query, key, value],
        [query],
    )

    attended_all = jnp.concatenate(
        [attended] + [over_zz(attended, j) for j in range(1, tp)], axis=0
    )
    out_partial = dot(attended_all, weight).astype(BF).reshape(tp, tokens, -1)
    out_sum = piece(out_partial, zz ^ t).astype(F32)
    for k in range(1, tp):
        out_sum += over_tensor(piece(out_partial, zz ^ t ^ k), k).astype(F32)
    cross_out = transposed(out_sum.astype(BF))

    grad_query, grad_key, grad_value = per_head(
        functools.partial(backward_kernel, spans, keys, scale),
        head_size,
        [query, key, value, grad_attended],
        [query, key, value],
    )

    states_partial = (dot_nt(grad_key, key_weight) + dot_nt(grad_value, value_weight)).astype(BF)
    states_partial = jnp.stack(jnp.split(states_partial, tp, axis=1))
    states_sum = piece(states_partial, t).astype(F32)
    for k in range(1, tp):
        states_sum += over_tensor(piece(states_partial, t ^ k), k).astype(F32)
    grad_rows = states_sum.astype(BF).reshape(block_count, block_len, width_part)
    low, high = grad_rows[:CAP], grad_rows[CAP:]
    returned = []
    for offset in range(1, WINDOW + 1):
        outgoing = jnp.where(owner_gap[CAP] == offset, high, low)
        returned.append(
            lax.ppermute(
                outgoing, "dp", [(i, (i + offset) % dp_count) for i in range(dp_count)]
            )
        )
    halves = []
    for k in range(block_count // CAP):
        picked = returned[0]
        for offset in range(2, WINDOW + 1):
            picked = jnp.where(target_gap[k * CAP] == offset, returned[offset - 1], picked)
        halves.append(picked)
    grad_states = jnp.concatenate(halves, axis=0)

    def hidden_piece(k):
        rows = lax.dynamic_slice_in_dim(query_weight, (t ^ k) * width, width, 0)
        return dot_nt(grad_query, rows).astype(BF)

    grad_hidden = hidden_piece(0).astype(F32)
    for k in range(1, tp):
        grad_hidden += over_tensor(hidden_piece(k), k).astype(F32)
    return (cross_out, grad_hidden.astype(BF), grad_states)


def solution(mesh):
    placed = (
        P("dp", "tensor"),
        P("dp", "tensor"),
        P(None, "tensor"),
        P(None, "tensor"),
        P(None, "tensor"),
        P("tensor", "dp"),
        P("dp", None, "tensor"),
        P("dp", None),
        P("dp", None),
    )
    return jax.shard_map(
        shards,
        mesh=mesh,
        in_specs=placed,
        out_specs=(P("dp", "tensor"), P("dp", "tensor"), P("dp", None, "tensor")),
        check_vma=False,
    )
```

```python
import functools
import math

import jax
import jax.numpy as jnp
from jax import lax
from jax.experimental import pallas as pl
from jax.experimental.pallas import tpu as pltpu
from jax.sharding import PartitionSpec as P

HEADS = 32
SPAN = 64
K_NB = 2
CAP = 2
WINDOW = 4
BF = jnp.bfloat16
F32 = jnp.float32


def dot_nt(left, right):
    return lax.dot_general(left, right, (((1,), (1,)), ((), ())), preferred_element_type=F32)


def dot_tn(left, right):
    return lax.dot_general(left, right, (((0,), (0,)), ((), ())), preferred_element_type=F32)


def dot(left, right):
    return jnp.dot(left, right, preferred_element_type=F32)


MESH = pl.DeviceIdType.MESH


def kernel(
    dp_count,
    tp,
    owner_ref,
    target_ref,
    hidden_ref,
    grad_ref,
    states_ref,
    wq_hbm,
    kw_hbm,
    vw_hbm,
    ow_hbm,
    cross_ref,
    gh_ref,
    gst_ref,
    wq,
    kw,
    vw,
    w,
    hid,
    turned,
    ga_send,
    ga_recv,
    out_blocks,
    arrived,
    nb,
    q_s,
    k_s,
    v_s,
    att,
    probs_s,
    ga_s,
    gq_s,
    gk_s,
    gv_s,
    st_send,
    st_recv,
    rows_s,
    ret_send,
    ret_recv,
    hp_send,
    hp_recv,
    cp_send,
    cp_recv,
    co_mine,
    co_last,
    send_sem,
    recv_sem,
    local_sem,
):
    g = dp_count // tp
    d, t = lax.axis_index("dp"), lax.axis_index("tensor")
    zz, gx = d // g, d % g
    tokens, width = hidden_ref.shape
    block_count, block_len, width_part = states_ref.shape
    rows_all = block_count * block_len
    pair_rows = CAP * block_len
    pairs = block_count // CAP
    cols = w.shape[2]
    local = q_s.shape[1]
    head_size = local * tp // HEADS
    scale = 1.0 / math.sqrt(head_size)
    spans = tokens // SPAN
    keys = K_NB * block_len

    def tensor_peer(k):
        return (d, (t + k) % tp)

    def zz_peer(j):
        return ((zz + j) % tp * g + gx, t)

    def group_peer(k):
        return (zz * g + (gx + k) % g, t)

    def dp_peer(o):
        return ((d + o + dp_count) % dp_count, t)

    turn_peer = (t * g + gx, zz)
    on_diagonal = t == zz

    local_copies = []

    def load(src, dst):
        copy = pltpu.make_async_copy(src, dst, local_sem.at[len(local_copies)])
        copy.start()
        local_copies.append(copy)
        return copy

    load_w = load(ow_hbm, w.at[gx])
    load_q, load_k, load_v = [], [], []
    for k in range(tp):
        load_q.append(load(wq_hbm.at[pl.ds((t + tp - k) % tp * width, width), :], wq.at[k]))
    for k in range(tp):
        rows = pl.ds((t + tp - k) % tp * width_part, width_part)
        load_k.append(load(kw_hbm.at[rows, :], kw.at[k]))
        load_v.append(load(vw_hbm.at[rows, :], vw.at[k]))

    barrier = pltpu.get_barrier_semaphore()
    peers = [tensor_peer(k) for k in range(1, tp)] + [zz_peer(j) for j in range(1, tp)]
    peers += [group_peer(k) for k in range(1, g)]
    peers += [dp_peer(o) for o in range(1, WINDOW + 1)]
    peers += [dp_peer(-o) for o in range(1, WINDOW + 1)]
    peers.append(turn_peer)
    for peer in peers:
        pl.semaphore_signal(barrier, inc=1, device_id=peer, device_id_type=MESH)
    pl.semaphore_wait(barrier, len(peers))

    sent = []
    used = [0]

    def remote(src, dst, peer):
        i = used[0]
        used[0] += 1
        return pltpu.make_async_remote_copy(
            src_ref=src,
            dst_ref=dst,
            send_sem=send_sem.at[i],
            recv_sem=recv_sem.at[i],
            device_id=peer,
            device_id_type=MESH,
        )

    def send(src, dst, peer):
        copy = remote(src, dst, peer)
        copy.start()
        sent.append(copy)
        return copy

    def is_gap(gap, o):
        return jnp.where(gap == o, 1.0, 0.0).astype(F32)

    owner_gap = [(owner_ref[0, k * CAP] - d + dp_count) % dp_count for k in range(pairs)]
    target_gap = [(d - target_ref[0, k * CAP] + dp_count) % dp_count for k in range(pairs)]

    for o in range(1, WINDOW + 1):
        block = sum(
            is_gap(target_gap[k], o)
            * states_ref[pl.ds(k * CAP, CAP)].astype(F32).reshape(pair_rows, width_part)
            for k in range(pairs)
        )
        out_blocks[o - 1] = block.astype(BF)
    blocks_in = [
        send(out_blocks.at[o - 1], arrived.at[o - 1], dp_peer(-o)) for o in range(1, WINDOW + 1)
    ]
    turn_in = remote(grad_ref, turned.at[0], turn_peer)

    @pl.when(jnp.logical_not(on_diagonal))
    def _():
        turn_in.start()

    @pl.when(on_diagonal)
    def _():
        turned[0] = grad_ref[...]

    hidden_in = [None] + [send(hidden_ref, hid.at[k], tensor_peer(k)) for k in range(1, tp)]
    weight_in = [send(ow_hbm, w.at[gx], group_peer(k)) for k in range(1, g)]

    for copy in blocks_in:
        copy.wait_recv()
    for k in range(pairs):
        block = sum(
            is_gap(owner_gap[k], o) * arrived[o - 1].astype(F32) for o in range(1, WINDOW + 1)
        )
        nb[0, pl.ds(k * pair_rows, pair_rows), :] = block.astype(BF)
    nb_in = [None] + [send(nb.at[0], nb.at[k], tensor_peer(k)) for k in range(1, tp)]

    @pl.when(jnp.logical_not(on_diagonal))
    def _():
        turn_in.wait()

    turned_in = [send(turned.at[0], turned.at[k], tensor_peer(k)) for k in range(1, tp)]

    hid[0] = hidden_ref[...]
    for k in range(1, tp):
        hidden_in[k].wait_recv()
    for copy in load_q:
        copy.wait()
    tile = min(256, local)
    for c in range(0, local, tile):
        at = pl.ds(c, tile)
        q_s[:, at] = sum(dot(hid[k], wq[k, :, at]) for k in range(tp)).astype(BF)

    load_w.wait()
    for copy in weight_in + turned_in:
        copy.wait_recv()

    def ga_partial(j):
        block = turned[(t - zz - j + 2 * tp) % tp]
        return sum(
            dot_nt(block[:, m * cols : (m + 1) * cols], w[m]) for m in range(g)
        )

    ga_in = []
    for j in range(1, tp):
        ga_send[j] = ga_partial(j).astype(BF)
        ga_in.append(send(ga_send.at[j], ga_recv.at[j], zz_peer(j)))
    ga_send[0] = ga_partial(0).astype(BF)

    for k in range(1, tp):
        nb_in[k].wait_recv()
    for copy in load_k + load_v:
        copy.wait()
    for c in range(0, local, tile):
        at = pl.ds(c, tile)
        k_s[:, at] = sum(dot(nb[k], kw[k, :, at]) for k in range(tp)).astype(BF)
        v_s[:, at] = sum(dot(nb[k], vw[k, :, at]) for k in range(tp)).astype(BF)

    heads = local // head_size

    def forward(h, carry):
        at = pl.ds(pl.multiple_of(h * head_size, head_size), head_size)
        for c in range(spans):
            mine, theirs = pl.ds(c * SPAN, SPAN), pl.ds(c * keys, keys)
            scores = dot_nt(q_s[mine, at], k_s[theirs, at]) * scale
            expanded = jnp.exp(scores - jnp.max(scores, axis=-1, keepdims=True))
            probs = expanded / jnp.sum(expanded, axis=-1, keepdims=True)
            probs_s[h, mine, :] = probs
            att[0, mine, at] = dot(probs.astype(BF), v_s[theirs, at]).astype(BF)
        return carry

    lax.fori_loop(0, heads, forward, 0)
    att_in = [send(att.at[0], att.at[j], zz_peer(j)) for j in range(1, tp)]

    for copy in ga_in:
        copy.wait_recv()
    total = ga_send[0].astype(F32)
    for j in range(1, tp):
        total += ga_recv[j].astype(F32)
    ga_s[...] = total.astype(BF)

    def backward(h, carry):
        at = pl.ds(pl.multiple_of(h * head_size, head_size), head_size)
        for c in range(spans):
            mine, theirs = pl.ds(c * SPAN, SPAN), pl.ds(c * keys, keys)
            probs, ga = probs_s[h, mine, :], ga_s[mine, at]
            gp = dot_nt(ga, v_s[theirs, at])
            gs = (probs * (gp - jnp.sum(probs * gp, axis=-1, keepdims=True)) * scale).astype(BF)
            gq_s[mine, at] = dot(gs, k_s[theirs, at]).astype(BF)
            gk_s[theirs, at] = dot_tn(gs, q_s[mine, at]).astype(BF)
            gv_s[theirs, at] = dot_tn(probs.astype(BF), ga).astype(BF)
        return carry

    lax.fori_loop(0, heads, backward, 0)

    def states_partial(k):
        slot = (tp - k) % tp
        return dot_nt(gk_s[...], kw[slot]) + dot_nt(gv_s[...], vw[slot])

    st_in = []
    for k in range(1, tp):
        st_send[k] = states_partial(k).astype(BF)
        st_in.append(send(st_send.at[k], st_recv.at[k], tensor_peer(k)))
    st_send[0] = states_partial(0).astype(BF)

    for copy in att_in:
        copy.wait_recv()

    def cross_partial(k):
        block = att[(zz - t - k + 2 * tp) % tp]
        for m in range(g):
            cp_send[k, :, m * cols : (m + 1) * cols] = dot(block, w[m]).astype(BF)

    cp_in = []
    for k in range(1, tp):
        cross_partial(k)
        cp_in.append(send(cp_send.at[k], cp_recv.at[k], tensor_peer(k)))
    cross_partial(0)

    def hidden_partial(k):
        return dot_nt(gq_s[...], wq[(tp - k) % tp])

    hp_in = []
    for k in range(1, tp):
        hp_send[k] = hidden_partial(k).astype(BF)
        hp_in.append(send(hp_send.at[k], hp_recv.at[k], tensor_peer(k)))

    for copy in st_in:
        copy.wait_recv()
    total = st_send[0].astype(F32)
    for k in range(1, tp):
        total += st_recv[k].astype(F32)
    rows_s[...] = total.astype(BF)
    for o in range(1, WINDOW + 1):
        block = sum(
            is_gap(owner_gap[k], o) * rows_s[pl.ds(k * pair_rows, pair_rows), :].astype(F32)
            for k in range(pairs)
        )
        ret_send[o - 1] = block.astype(BF)
    ret_in = [
        send(ret_send.at[o - 1], ret_recv.at[o - 1], dp_peer(o)) for o in range(1, WINDOW + 1)
    ]

    for copy in cp_in:
        copy.wait_recv()
    total = cp_send[0].astype(F32)
    for k in range(1, tp):
        total += cp_recv[k].astype(F32)
    co_mine[...] = total.astype(BF)
    cross_in = remote(co_mine, co_last, turn_peer)

    @pl.when(jnp.logical_not(on_diagonal))
    def _():
        cross_in.start()

    @pl.when(on_diagonal)
    def _():
        co_last[...] = co_mine[...]

    total = hidden_partial(0).astype(BF).astype(F32)
    for copy in hp_in:
        copy.wait_recv()
    for k in range(1, tp):
        total += hp_recv[k].astype(F32)
    gh_ref[...] = total.astype(BF)

    for copy in ret_in:
        copy.wait_recv()
    for k in range(pairs):
        block = sum(
            is_gap(target_gap[k], o) * ret_recv[o - 1].astype(F32) for o in range(1, WINDOW + 1)
        )
        gst_ref[pl.ds(k * CAP, CAP)] = block.astype(BF).reshape(CAP, block_len, width_part)

    @pl.when(jnp.logical_not(on_diagonal))
    def _():
        cross_in.wait()

    cross_ref[...] = co_last[...]
    for copy in sent:
        copy.wait_send()


def shards(
    hidden,
    grad_out,
    query_weight,
    key_weight,
    value_weight,
    out_weight,
    neighbour_states,
    block_owner,
    slot_target,
):
    dp_count, tp = lax.axis_size("dp"), lax.axis_size("tensor")
    g = dp_count // tp
    tokens, width = hidden.shape
    local = query_weight.shape[1]
    block_count, block_len, width_part = neighbour_states.shape
    rows = block_count * block_len
    pair_rows = CAP * block_len
    heads = HEADS // tp
    copies = 2 * WINDOW + 8 * (tp - 1) + (g - 1) + 2

    def vmem(*shape, kind=BF):
        return pltpu.VMEM(shape, kind)

    in_vmem = pl.BlockSpec(memory_space=pltpu.VMEM)
    in_smem = pl.BlockSpec(memory_space=pltpu.SMEM)
    anywhere = pl.BlockSpec(memory_space=pl.ANY)
    multiply_adds = tokens * tp * width * local * 4 + rows * local * tp * width_part * 4
    return pl.pallas_call(
        functools.partial(kernel, dp_count, tp),
        in_specs=[in_smem] * 2 + [in_vmem] * 3 + [anywhere] * 4,
        out_specs=[in_vmem] * 3,
        out_shape=[
            jax.ShapeDtypeStruct(hidden.shape, BF),
            jax.ShapeDtypeStruct(hidden.shape, BF),
            jax.ShapeDtypeStruct(neighbour_states.shape, BF),
        ],
        scratch_shapes=[
            vmem(tp, width, local),
            vmem(tp, width_part, local),
            vmem(tp, width_part, local),
            vmem(g, *out_weight.shape),
            vmem(tp, tokens, width),
            vmem(tp, tokens, width),
            vmem(tp, tokens, local),
            vmem(tp, tokens, local),
            vmem(WINDOW, pair_rows, width_part),
            vmem(WINDOW, pair_rows, width_part),
            vmem(tp, rows, width_part),
            vmem(tokens, local),
            vmem(rows, local),
            vmem(rows, local),
            vmem(tp, tokens, local),
            vmem(heads, tokens, K_NB * block_len, kind=F32),
            vmem(tokens, local),
            vmem(tokens, local),
            vmem(rows, local),
            vmem(rows, local),
            vmem(tp, rows, width_part),
            vmem(tp, rows, width_part),
            vmem(rows, width_part),
            vmem(WINDOW, pair_rows, width_part),
            vmem(WINDOW, pair_rows, width_part),
            vmem(tp, tokens, width),
            vmem(tp, tokens, width),
            vmem(tp, tokens, width),
            vmem(tp, tokens, width),
            vmem(tokens, width),
            vmem(tokens, width),
            pltpu.SemaphoreType.DMA((copies,)),
            pltpu.SemaphoreType.DMA((copies,)),
            pltpu.SemaphoreType.DMA((3 * tp + 1,)),
        ],
        cost_estimate=pl.CostEstimate(
            flops=2 * multiply_adds, bytes_accessed=16 * 2**20, transcendentals=0
        ),
        compiler_params=pltpu.CompilerParams(
            collective_id=0, has_side_effects=True, vmem_limit_bytes=52 * 2**20
        ),
    )(
        block_owner,
        slot_target,
        hidden,
        grad_out,
        neighbour_states,
        query_weight,
        key_weight,
        value_weight,
        out_weight,
    )


def solution(mesh):
    placed = (
        P("dp", "tensor"),
        P("dp", "tensor"),
        P(None, "tensor"),
        P(None, "tensor"),
        P(None, "tensor"),
        P("tensor", "dp"),
        P("dp", None, "tensor"),
        P("dp", None),
        P("dp", None),
    )
    return jax.shard_map(
        shards,
        mesh=mesh,
        in_specs=placed,
        out_specs=(P("dp", "tensor"), P("dp", "tensor"), P("dp", None, "tensor")),
        check_vma=False,
    )
```

```python
import functools
import math

import jax
import jax.numpy as jnp
from jax import lax
from jax.experimental import pallas as pl
from jax.experimental.pallas import tpu as pltpu
from jax.sharding import PartitionSpec as P

HEADS = 32
SPAN = 64
K_NB = 2
CAP = 2
WINDOW = 4
BF = jnp.bfloat16
F32 = jnp.float32


def dot_nt(left, right):
    return lax.dot_general(left, right, (((1,), (1,)), ((), ())), preferred_element_type=F32)


def dot_tn(left, right):
    return lax.dot_general(left, right, (((0,), (0,)), ((), ())), preferred_element_type=F32)


def dot(left, right):
    return jnp.dot(left, right, preferred_element_type=F32)


MESH = pl.DeviceIdType.MESH
LANES = 128


def flip(i, k):
    if k % 2:
        i = i + 1 - 2 * (i % 2)
    return (i + 2) % 4 if k >= 2 else i


def packed(block):
    half = block.shape[0] // 2
    rest = jnp.concatenate([block[:half, LANES:], block[half:, LANES:]], axis=1)
    return jnp.concatenate([block[:, :LANES], rest], axis=0)


def kernel(
    dp_count,
    tp,
    owner_hbm,
    target_hbm,
    hidden_hbm,
    grad_hbm,
    states_hbm,
    wq_hbm,
    kw_hbm,
    vw_hbm,
    ow_hbm,
    cross_ref,
    gh_ref,
    gst_ref,
    owner_ref,
    target_ref,
    states_ref,
    wq,
    kw,
    vw,
    w,
    hid,
    turned,
    ga_send,
    ga_recv,
    out_blocks,
    arrived,
    nbp,
    nb,
    q_s,
    k_s,
    v_s,
    att,
    probs_s,
    ga_s,
    gq_s,
    gk_s,
    gv_s,
    st_send,
    st_recv,
    rows_s,
    ret_send,
    ret_recv,
    hp_send,
    hp_recv,
    cp_send,
    cp_recv,
    co_mine,
    co_last,
    send_sem,
    recv_sem,
    local_sem,
):
    g = dp_count // tp
    d, t = lax.axis_index("dp"), lax.axis_index("tensor")
    zz, gx = d // g, d % g
    tokens, width = hidden_hbm.shape
    block_count, block_len, width_part = states_ref.shape
    rows_all = block_count * block_len
    pair_rows = CAP * block_len
    pairs = block_count // CAP
    cols = w.shape[2]
    local = q_s.shape[1]
    head_size = local * tp // HEADS
    scale = 1.0 / math.sqrt(head_size)
    spans = tokens // SPAN
    keys = K_NB * block_len

    def tensor_peer(k):
        return (d, flip(t, k))

    def zz_peer(j):
        return (flip(zz, j) * g + gx, t)

    def group_peer(k):
        return (zz * g + (gx + k) % g, t)

    def dp_peer(o):
        return ((d + o + dp_count) % dp_count, t)

    turn_peer = (t * g + gx, zz)
    on_diagonal = t == zz
    apart = (zz + t) % 2 + 2 * ((zz // 2 + t // 2) % 2)

    local_copies = []

    def load(src, dst):
        copy = pltpu.make_async_copy(src, dst, local_sem.at[len(local_copies)])
        copy.start()
        local_copies.append(copy)
        return copy

    load_small = [
        load(owner_hbm, owner_ref),
        load(target_hbm, target_ref),
        load(states_hbm, states_ref),
    ]
    load_hidden = load(hidden_hbm, hid.at[0])
    load_w = load(ow_hbm, w.at[gx])
    load_q, load_kv = [], []
    for k in range(tp):
        load_q.append(load(wq_hbm.at[pl.ds(flip(t, k) * width, width), :], wq.at[k]))
    rest = width_part - LANES
    for k in range(tp):
        for hbm, here in ((kw_hbm, kw), (vw_hbm, vw)):
            start = flip(t, k) * width_part
            for first, size, to in ((0, LANES, k * LANES), (LANES, rest, tp * LANES + k * rest)):
                load_kv.append(
                    load(hbm.at[pl.ds(start + first, size), :], here.at[pl.ds(to, size), :])
                )

    barrier = pltpu.get_barrier_semaphore()
    peers = [tensor_peer(1), tensor_peer(2), zz_peer(1), zz_peer(2)]
    peers += [group_peer(k) for k in range(1, g)]
    peers += [dp_peer(o) for o in range(1, WINDOW + 1)]
    peers += [dp_peer(-o) for o in range(1, WINDOW + 1)]
    peers.append(turn_peer)
    for peer in peers:
        pl.semaphore_signal(barrier, inc=1, device_id=peer, device_id_type=MESH)
    pl.semaphore_wait(barrier, len(peers))

    sent = []
    used = [0]

    def remote(src, dst, peer):
        i = used[0]
        used[0] += 1
        return pltpu.make_async_remote_copy(
            src_ref=src,
            dst_ref=dst,
            send_sem=send_sem.at[i],
            recv_sem=recv_sem.at[i],
            device_id=peer,
            device_id_type=MESH,
        )

    def send(src, dst, peer):
        copy = remote(src, dst, peer)
        copy.start()
        sent.append(copy)
        return copy

    def gather(src, slots, peer):
        return [send(src, slots.at[1], peer(1)), send(src, slots.at[2], peer(2))]

    def forwarded(slots, peer, copies):
        copies[1].wait_recv()
        return send(slots.at[2], slots.at[3], peer(1))

    def scatter_start(parts, recv, peer):
        return [send(parts.at[3], recv.at[1], peer(1)), send(parts.at[1], recv.at[0], peer(1))]

    def scatter_middle(parts, recv, peer, copies):
        copies[0].wait_recv()
        parts[2] = (parts[2].astype(F32) + recv[1].astype(F32)).astype(BF)
        copies.append(send(parts.at[2], recv.at[2], peer(2)))

    def scatter_end(parts, recv, copies):
        copies[1].wait_recv()
        copies[2].wait_recv()
        return parts[0].astype(F32) + recv[0].astype(F32) + recv[2].astype(F32)

    def is_gap(gap, o):
        return jnp.where(gap == o, 1.0, 0.0).astype(F32)

    for copy in load_small:
        copy.wait()
    owner_gap = [(owner_ref[0, k * CAP] - d + dp_count) % dp_count for k in range(pairs)]
    target_gap = [(d - target_ref[0, k * CAP] + dp_count) % dp_count for k in range(pairs)]

    pair_packs = [
        packed(states_ref[pl.ds(k * CAP, CAP)].astype(F32).reshape(pair_rows, width_part))
        for k in range(pairs)
    ]
    blocks_in = []
    for o in range(1, WINDOW + 1):
        block = sum(is_gap(target_gap[k], o) * pair_packs[k] for k in range(pairs))
        out_blocks[o - 1] = block.astype(BF)
        blocks_in.append(send(out_blocks.at[o - 1], arrived.at[o - 1], dp_peer(-o)))
    turn_in = remote(grad_hbm, turned.at[0], turn_peer)
    turn_local = pltpu.make_async_copy(grad_hbm, turned.at[0], local_sem.at[len(local_copies)])

    @pl.when(jnp.logical_not(on_diagonal))
    def _():
        turn_in.start()

    @pl.when(on_diagonal)
    def _():
        turn_local.start()

    hidden_in = gather(hidden_hbm, hid, tensor_peer)
    weight_in = [send(ow_hbm, w.at[gx], group_peer(k)) for k in range(1, g)]

    @pl.when(jnp.logical_not(on_diagonal))
    def _():
        turn_in.wait()

    @pl.when(on_diagonal)
    def _():
        turn_local.wait()

    turned_in = gather(turned.at[0], turned, tensor_peer)

    for copy in blocks_in:
        copy.wait_recv()
    for k in range(pairs):
        block = sum(
            is_gap(owner_gap[k], o) * arrived[o - 1].astype(F32) for o in range(1, WINDOW + 1)
        ).astype(BF)
        nbp[0, pl.ds(k * pair_rows, pair_rows), :] = block[:pair_rows]
        nbp[0, pl.ds(rows_all + k * block_len, block_len), :] = block[pair_rows:]
    nb_in = gather(nbp.at[0], nbp, tensor_peer)

    hidden_in.append(forwarded(hid, tensor_peer, hidden_in))
    turned_in.append(forwarded(turned, tensor_peer, turned_in))
    load_hidden.wait()
    hidden_in[0].wait_recv()
    hidden_in[2].wait_recv()
    for copy in load_q:
        copy.wait()
    tile = min(256, local)
    for c in range(0, local, tile):
        at = pl.ds(c, tile)
        q_s[:, at] = sum(dot(hid[k], wq[k, :, at]) for k in range(tp)).astype(BF)
    nb_in.append(forwarded(nbp, tensor_peer, nb_in))

    load_w.wait()
    for copy in weight_in:
        copy.wait_recv()
    turned_in[0].wait_recv()
    turned_in[2].wait_recv()

    def ga_partial(j):
        block = turned[flip(apart, j)]
        ga_send[j] = sum(
            dot_nt(block[:, m * cols : (m + 1) * cols], w[m]) for m in range(g)
        ).astype(BF)

    ga_partial(3)
    ga_partial(1)
    ga_in = scatter_start(ga_send, ga_recv, zz_peer)
    ga_partial(2)
    ga_partial(0)

    nb_in[0].wait_recv()
    nb_in[2].wait_recv()
    for k in range(tp):
        nb[:, k * LANES : (k + 1) * LANES] = nbp[k, pl.ds(0, rows_all), :]
    for k in range(0, tp, 2):
        for p in range(pairs):
            rows = pl.ds(rows_all + p * block_len, block_len)
            one, two = nbp[k, rows, :].astype(F32), nbp[k + 1, rows, :].astype(F32)
            lanes = pl.ds(tp * LANES + k * rest, 2 * rest)
            for half in range(2):
                part = slice(half * rest, (half + 1) * rest)
                joined = jnp.concatenate([one[:, part], two[:, part]], axis=1)
                nb[pl.ds((p * CAP + half) * block_len, block_len), lanes] = joined.astype(BF)
    for copy in load_kv:
        copy.wait()
    for c in range(0, local, tile):
        at = pl.ds(c, tile)
        k_s[:, at] = dot(nb[...], kw[:, at]).astype(BF)
        v_s[:, at] = dot(nb[...], vw[:, at]).astype(BF)
    scatter_middle(ga_send, ga_recv, zz_peer, ga_in)

    heads = local // head_size

    def forward(h, carry):
        at = pl.ds(pl.multiple_of(h * head_size, head_size), head_size)
        for c in range(spans):
            mine, theirs = pl.ds(c * SPAN, SPAN), pl.ds(c * keys, keys)
            scores = dot_nt(q_s[mine, at], k_s[theirs, at]) * scale
            expanded = jnp.exp(scores - jnp.max(scores, axis=-1, keepdims=True))
            probs = expanded / jnp.sum(expanded, axis=-1, keepdims=True)
            probs_s[h, mine, :] = probs
            att[0, mine, at] = dot(probs.astype(BF), v_s[theirs, at]).astype(BF)
        return carry

    lax.fori_loop(0, heads, forward, 0, unroll=4)
    att_in = gather(att.at[0], att, zz_peer)

    ga_s[...] = scatter_end(ga_send, ga_recv, ga_in).astype(BF)
    att_in.append(forwarded(att, zz_peer, att_in))

    def backward(h, carry):
        at = pl.ds(pl.multiple_of(h * head_size, head_size), head_size)
        for c in range(spans):
            mine, theirs = pl.ds(c * SPAN, SPAN), pl.ds(c * keys, keys)
            probs, ga = probs_s[h, mine, :], ga_s[mine, at]
            gp = dot_nt(ga, v_s[theirs, at])
            gs = (probs * (gp - jnp.sum(probs * gp, axis=-1, keepdims=True)) * scale).astype(BF)
            gq_s[mine, at] = dot(gs, k_s[theirs, at]).astype(BF)
            gk_s[theirs, at] = dot_tn(gs, q_s[mine, at]).astype(BF)
            gv_s[theirs, at] = dot_tn(probs.astype(BF), ga).astype(BF)
        return carry

    lax.fori_loop(0, heads, backward, 0, unroll=4)

    for k in range(0, tp, 2):
        at = pl.ds(k * LANES, 2 * LANES)
        both = dot_nt(gk_s[...], kw[at, :]) + dot_nt(gv_s[...], vw[at, :])
        for i in range(2):
            st_send[k + i, pl.ds(0, rows_all), :] = both[:, i * LANES : (i + 1) * LANES].astype(BF)
    at = pl.ds(tp * LANES, tp * rest)
    both = dot_nt(gk_s[...], kw[at, :]) + dot_nt(gv_s[...], vw[at, :])
    for k in range(tp):
        part = slice(k * rest, (k + 1) * rest)
        for p in range(pairs):
            top = p * pair_rows
            joined = jnp.concatenate(
                [both[top : top + block_len, part], both[top + block_len : top + pair_rows, part]],
                axis=1,
            )
            st_send[k, pl.ds(rows_all + p * block_len, block_len), :] = joined.astype(BF)
    st_in = scatter_start(st_send, st_recv, tensor_peer)

    def cross_partial(k):
        block = att[flip(apart, k)]
        for m in range(g):
            cp_send[k, :, m * cols : (m + 1) * cols] = dot(block, w[m]).astype(BF)

    att_in[0].wait_recv()
    att_in[2].wait_recv()
    cross_partial(3)
    cross_partial(1)
    cp_in = scatter_start(cp_send, cp_recv, tensor_peer)
    scatter_middle(st_send, st_recv, tensor_peer, st_in)
    cross_partial(2)
    scatter_middle(cp_send, cp_recv, tensor_peer, cp_in)
    cross_partial(0)

    def hidden_partial(k):
        hp_send[k] = dot_nt(gq_s[...], wq[k]).astype(BF)

    hidden_partial(3)
    hidden_partial(1)
    hp_in = scatter_start(hp_send, hp_recv, tensor_peer)

    rows_s[...] = scatter_end(st_send, st_recv, st_in).astype(BF)
    ret_in = []
    for o in range(1, WINDOW + 1):
        for first, size, to in ((0, pair_rows, 0), (rows_all, block_len, pair_rows)):
            block = sum(
                is_gap(owner_gap[k], o) * rows_s[pl.ds(first + k * size, size), :].astype(F32)
                for k in range(pairs)
            )
            ret_send[o - 1, pl.ds(to, size), :] = block.astype(BF)
        ret_in.append(send(ret_send.at[o - 1], ret_recv.at[o - 1], dp_peer(o)))

    co_mine[...] = scatter_end(cp_send, cp_recv, cp_in).astype(BF)
    cross_in = remote(co_mine, co_last, turn_peer)

    @pl.when(jnp.logical_not(on_diagonal))
    def _():
        cross_in.start()

    @pl.when(on_diagonal)
    def _():
        co_last[...] = co_mine[...]

    hidden_partial(2)
    scatter_middle(hp_send, hp_recv, tensor_peer, hp_in)
    hidden_partial(0)
    gh_ref[...] = scatter_end(hp_send, hp_recv, hp_in).astype(BF)

    for copy in ret_in:
        copy.wait_recv()
    for k in range(pairs):
        block = sum(
            is_gap(target_gap[k], o) * ret_recv[o - 1].astype(F32) for o in range(1, WINDOW + 1)
        )
        for i in range(CAP):
            gst_ref[k * CAP + i, :, :LANES] = block[i * block_len : (i + 1) * block_len].astype(BF)
            gst_ref[k * CAP + i, :, LANES:] = block[
                pair_rows:, i * rest : (i + 1) * rest
            ].astype(BF)

    @pl.when(jnp.logical_not(on_diagonal))
    def _():
        cross_in.wait()

    cross_ref[...] = co_last[...]
    for copy in sent:
        copy.wait_send()


def shards(
    hidden,
    grad_out,
    query_weight,
    key_weight,
    value_weight,
    out_weight,
    neighbour_states,
    block_owner,
    slot_target,
):
    dp_count, tp = lax.axis_size("dp"), lax.axis_size("tensor")
    g = dp_count // tp
    tokens, width = hidden.shape
    local = query_weight.shape[1]
    block_count, block_len, width_part = neighbour_states.shape
    rows = block_count * block_len
    pack = rows * width_part // LANES
    heads = HEADS // tp
    copies = 2 * WINDOW + 8 * (tp - 1) + (g - 1) + 2

    def vmem(*shape, kind=BF):
        return pltpu.VMEM(shape, kind)

    in_vmem = pl.BlockSpec(memory_space=pltpu.VMEM)
    anywhere = pl.BlockSpec(memory_space=pl.ANY)
    multiply_adds = tokens * tp * width * local * 4 + rows * local * tp * width_part * 4
    return pl.pallas_call(
        functools.partial(kernel, dp_count, tp),
        in_specs=[anywhere] * 9,
        out_specs=[in_vmem] * 3,
        out_shape=[
            jax.ShapeDtypeStruct(hidden.shape, BF),
            jax.ShapeDtypeStruct(hidden.shape, BF),
            jax.ShapeDtypeStruct(neighbour_states.shape, BF),
        ],
        scratch_shapes=[
            pltpu.SMEM(block_owner.shape, jnp.int32),
            pltpu.SMEM(slot_target.shape, jnp.int32),
            vmem(*neighbour_states.shape),
            vmem(tp, width, local),
            vmem(tp * width_part, local),
            vmem(tp * width_part, local),
            vmem(g, *out_weight.shape),
            vmem(tp, tokens, width),
            vmem(tp, tokens, width),
            vmem(tp, tokens, local),
            vmem(tp, tokens, local),
            vmem(WINDOW, 3 * block_len, LANES),
            vmem(WINDOW, 3 * block_len, LANES),
            vmem(tp, pack, LANES),
            vmem(rows, tp * width_part),
            vmem(tokens, local),
            vmem(rows, local),
            vmem(rows, local),
            vmem(tp, tokens, local),
            vmem(heads, tokens, K_NB * block_len, kind=F32),
            vmem(tokens, local),
            vmem(tokens, local),
            vmem(rows, local),
            vmem(rows, local),
            vmem(tp, pack, LANES),
            vmem(tp, pack, LANES),
            vmem(pack, LANES),
            vmem(WINDOW, 3 * block_len, LANES),
            vmem(WINDOW, 3 * block_len, LANES),
            vmem(tp, tokens, width),
            vmem(tp, tokens, width),
            vmem(tp, tokens, width),
            vmem(tp, tokens, width),
            vmem(tokens, width),
            vmem(tokens, width),
            pltpu.SemaphoreType.DMA((copies,)),
            pltpu.SemaphoreType.DMA((copies,)),
            pltpu.SemaphoreType.DMA((5 * tp + 6,)),
        ],
        cost_estimate=pl.CostEstimate(
            flops=2 * multiply_adds, bytes_accessed=16 * 2**20, transcendentals=0
        ),
        compiler_params=pltpu.CompilerParams(
            collective_id=0, has_side_effects=True, vmem_limit_bytes=52 * 2**20
        ),
    )(
        block_owner,
        slot_target,
        hidden,
        grad_out,
        neighbour_states,
        query_weight,
        key_weight,
        value_weight,
        out_weight,
    )


def solution(mesh):
    placed = (
        P("dp", "tensor"),
        P("dp", "tensor"),
        P(None, "tensor"),
        P(None, "tensor"),
        P(None, "tensor"),
        P("tensor", "dp"),
        P("dp", None, "tensor"),
        P("dp", None),
        P("dp", None),
    )
    return jax.shard_map(
        shards,
        mesh=mesh,
        in_specs=placed,
        out_specs=(P("dp", "tensor"), P("dp", "tensor"), P("dp", None, "tensor")),
        check_vma=False,
    )
```

```python
import functools
import math

import jax
import jax.numpy as jnp
from jax import lax
from jax.experimental import pallas as pl
from jax.experimental.pallas import tpu as pltpu
from jax.sharding import PartitionSpec as P

HEADS = 32
SPAN = 64
K_NB = 2
CAP = 2
WINDOW = 4
BF = jnp.bfloat16
F32 = jnp.float32


def dot_nt(left, right):
    return lax.dot_general(left, right, (((1,), (1,)), ((), ())), preferred_element_type=F32)


def dot_tn(left, right):
    return lax.dot_general(left, right, (((0,), (0,)), ((), ())), preferred_element_type=F32)


def dot(left, right):
    return jnp.dot(left, right, preferred_element_type=F32)


MESH = pl.DeviceIdType.MESH
PARTS = 2


def flip(i, k):
    if k % 2:
        i = i + 1 - 2 * (i % 2)
    return (i + 2) % 4 if k >= 2 else i


def kernel(
    dp_count,
    tp,
    owner_hbm,
    target_hbm,
    hidden_hbm,
    grad_hbm,
    states_hbm,
    wq_hbm,
    kw_hbm,
    vw_hbm,
    ow_hbm,
    cross_ref,
    gh_ref,
    gst_ref,
    owner_ref,
    target_ref,
    states_ref,
    wq,
    kw,
    vw,
    w,
    hid,
    turned,
    ga_send,
    ga_recv,
    out_blocks,
    arrived,
    nbp,
    nb,
    q_s,
    k_s,
    v_s,
    att,
    probs_s,
    ga_s,
    gq_s,
    gk_s,
    gv_s,
    st_send,
    st_recv,
    rows_s,
    ret_send,
    ret_recv,
    hp_send,
    hp_recv,
    cp_send,
    cp_recv,
    co_mine,
    co_last,
    send_sem,
    recv_sem,
    local_sem,
):
    g = dp_count // tp
    d, t = lax.axis_index("dp"), lax.axis_index("tensor")
    zz, gx = d // g, d % g
    tokens, width = hidden_hbm.shape
    block_count, width_part, block_len = states_ref.shape
    rows_all = block_count * block_len
    pair_rows = CAP * block_len
    pairs = block_count // CAP
    part = q_s.shape[1] // PARTS
    cols = w.shape[2]
    local = q_s.shape[1]
    head_size = local * tp // HEADS
    scale = 1.0 / math.sqrt(head_size)
    spans = tokens // SPAN
    keys = K_NB * block_len

    def tensor_peer(k):
        return (d, flip(t, k))

    def zz_peer(j):
        return (flip(zz, j) * g + gx, t)

    def group_peer(k):
        return (zz * g + (gx + k) % g, t)

    def dp_peer(o):
        return ((d + o + dp_count) % dp_count, t)

    turn_peer = (t * g + gx, zz)
    on_diagonal = t == zz
    apart = (zz + t) % 2 + 2 * ((zz // 2 + t // 2) % 2)

    local_copies = []

    def load(src, dst):
        copy = pltpu.make_async_copy(src, dst, local_sem.at[len(local_copies)])
        copy.start()
        local_copies.append(copy)
        return copy

    load_small = [
        load(owner_hbm, owner_ref),
        load(target_hbm, target_ref),
        load(states_hbm, states_ref),
    ]
    load_hidden = load(hidden_hbm, hid.at[0])
    load_w = load(ow_hbm, w.at[gx])
    load_q, load_kv = [], []
    for k in range(tp):
        load_q.append(load(wq_hbm.at[pl.ds(flip(t, k) * width, width), :], wq.at[k]))
    for k in range(tp):
        for hbm, here in ((kw_hbm, kw), (vw_hbm, vw)):
            rows = pl.ds(flip(t, k) * width_part, width_part)
            load_kv.append(load(hbm.at[rows, :], here.at[pl.ds(k * width_part, width_part), :]))

    barrier = pltpu.get_barrier_semaphore()
    peers = [tensor_peer(1), tensor_peer(2), zz_peer(1), zz_peer(2)]
    peers += [group_peer(k) for k in range(1, g)]
    peers += [dp_peer(o) for o in range(1, WINDOW + 1)]
    peers += [dp_peer(-o) for o in range(1, WINDOW + 1)]
    peers.append(turn_peer)
    for peer in peers:
        pl.semaphore_signal(barrier, inc=1, device_id=peer, device_id_type=MESH)
    pl.semaphore_wait(barrier, len(peers))

    sent = []
    used = [0]

    def remote(src, dst, peer):
        i = used[0]
        used[0] += 1
        return pltpu.make_async_remote_copy(
            src_ref=src,
            dst_ref=dst,
            send_sem=send_sem.at[i],
            recv_sem=recv_sem.at[i],
            device_id=peer,
            device_id_type=MESH,
        )

    def send(src, dst, peer):
        copy = remote(src, dst, peer)
        copy.start()
        sent.append(copy)
        return copy

    def gather(src, slots, peer):
        return [send(src, slots.at[1], peer(1)), send(src, slots.at[2], peer(2))]

    def forwarded(slots, peer, copies):
        copies[1].wait_recv()
        return send(slots.at[2], slots.at[3], peer(1))

    def scatter_start(parts, recv, peer):
        return [send(parts.at[3], recv.at[1], peer(1)), send(parts.at[1], recv.at[0], peer(1))]

    def scatter_middle(parts, recv, peer, copies):
        copies[0].wait_recv()
        parts[2] = (parts[2].astype(F32) + recv[1].astype(F32)).astype(BF)
        copies.append(send(parts.at[2], recv.at[2], peer(2)))

    def scatter_end(parts, recv, copies):
        copies[1].wait_recv()
        copies[2].wait_recv()
        return parts[0].astype(F32) + recv[0].astype(F32) + recv[2].astype(F32)

    def is_gap(gap, o):
        return jnp.where(gap == o, 1.0, 0.0).astype(F32)

    turn_in = remote(grad_hbm, turned.at[0], turn_peer)
    turn_local = pltpu.make_async_copy(grad_hbm, turned.at[0], local_sem.at[len(local_copies)])

    @pl.when(jnp.logical_not(on_diagonal))
    def _():
        turn_in.start()

    @pl.when(on_diagonal)
    def _():
        turn_local.start()

    def send_weight(h):
        rows = pl.ds(h * part, part)
        return [
            send(ow_hbm.at[rows, :], w.at[gx, rows, :], group_peer(k)) for k in range(1, g)
        ]

    weight_in = [send_weight(0)]
    hidden_in = gather(hidden_hbm, hid, tensor_peer)
    weight_in += [send_weight(h) for h in range(1, PARTS)]

    for copy in load_small:
        copy.wait()
    owner_gap = [(owner_ref[0, k * CAP] - d + dp_count) % dp_count for k in range(pairs)]
    target_gap = [(d - target_ref[0, k * CAP] + dp_count) % dp_count for k in range(pairs)]
    blocks_in = []
    for o in range(1, WINDOW + 1):
        for i in range(CAP):
            block = sum(
                is_gap(target_gap[k], o) * states_ref[k * CAP + i].astype(F32)
                for k in range(pairs)
            )
            out_blocks[o - 1, :, i * block_len : (i + 1) * block_len] = block.astype(BF)
        blocks_in.append(send(out_blocks.at[o - 1], arrived.at[o - 1], dp_peer(-o)))

    @pl.when(jnp.logical_not(on_diagonal))
    def _():
        turn_in.wait()

    @pl.when(on_diagonal)
    def _():
        turn_local.wait()

    turned_in = gather(turned.at[0], turned, tensor_peer)

    for copy in blocks_in:
        copy.wait_recv()
    for k in range(pairs):
        block = sum(
            is_gap(owner_gap[k], o) * arrived[o - 1].astype(F32) for o in range(1, WINDOW + 1)
        )
        nbp[0, :, k * pair_rows : (k + 1) * pair_rows] = block.astype(BF)
    nb_in = gather(nbp.at[0], nbp, tensor_peer)

    hidden_in.append(forwarded(hid, tensor_peer, hidden_in))
    turned_in.append(forwarded(turned, tensor_peer, turned_in))
    load_hidden.wait()
    hidden_in[0].wait_recv()
    hidden_in[2].wait_recv()
    for copy in load_q:
        copy.wait()
    tile = min(256, local)
    for c in range(0, local, tile):
        at = pl.ds(c, tile)
        q_s[:, at] = sum(dot(hid[k], wq[k, :, at]) for k in range(tp)).astype(BF)
    nb_in.append(forwarded(nbp, tensor_peer, nb_in))

    load_w.wait()
    turned_in[0].wait_recv()
    turned_in[2].wait_recv()

    def ga_partial(h, j):
        block = turned[flip(apart, j)]
        ga_send[h, j] = sum(
            dot_nt(block[:, m * cols : (m + 1) * cols], w[m, h * part : (h + 1) * part, :])
            for m in range(g)
        ).astype(BF)

    def ga_start(h):
        for copy in weight_in[h]:
            copy.wait_recv()
        ga_partial(h, 3)
        ga_partial(h, 1)
        copies = scatter_start(ga_send.at[h], ga_recv.at[h], zz_peer)
        ga_partial(h, 2)
        ga_partial(h, 0)
        return copies

    ga_in = [ga_start(0)]

    nb_in[0].wait_recv()
    nb_in[2].wait_recv()
    for b in range(block_count):
        block = nbp[:, :, b * block_len : (b + 1) * block_len]
        nb[b * block_len : (b + 1) * block_len, :] = block.reshape(tp * width_part, block_len).T
    for copy in load_kv:
        copy.wait()
    for c in range(0, local, tile):
        at = pl.ds(c, tile)
        k_s[:, at] = dot(nb[...], kw[:, at]).astype(BF)
        v_s[:, at] = dot(nb[...], vw[:, at]).astype(BF)
    scatter_middle(ga_send.at[0], ga_recv.at[0], zz_peer, ga_in[0])
    ga_in += [ga_start(h) for h in range(1, PARTS)]

    heads = local // head_size // PARTS

    def forward(first, n, carry):
        h = first + n
        at = pl.ds(pl.multiple_of(h * head_size, head_size), head_size)
        to = pl.ds(pl.multiple_of(n * head_size, head_size), head_size)
        for c in range(spans):
            mine, theirs = pl.ds(c * SPAN, SPAN), pl.ds(c * keys, keys)
            scores = dot_nt(q_s[mine, at], k_s[theirs, at]) * scale
            expanded = jnp.exp(scores - jnp.max(scores, axis=-1, keepdims=True))
            probs = expanded / jnp.sum(expanded, axis=-1, keepdims=True)
            probs_s[h, mine, :] = probs
            att[first // heads, 0, mine, to] = dot(probs.astype(BF), v_s[theirs, at]).astype(BF)
        return carry

    att_in = []
    for h in range(PARTS):
        lax.fori_loop(0, heads, functools.partial(forward, h * heads), 0, unroll=heads)
        att_in.append(gather(att.at[h, 0], att.at[h], zz_peer))
        if h:
            scatter_middle(ga_send.at[h], ga_recv.at[h], zz_peer, ga_in[h])

    def backward(first, n, carry):
        h = first + n
        at = pl.ds(pl.multiple_of(h * head_size, head_size), head_size)
        for c in range(spans):
            mine, theirs = pl.ds(c * SPAN, SPAN), pl.ds(c * keys, keys)
            probs, ga = probs_s[h, mine, :], ga_s[mine, at]
            gp = dot_nt(ga, v_s[theirs, at])
            gs = (probs * (gp - jnp.sum(probs * gp, axis=-1, keepdims=True)) * scale).astype(BF)
            gq_s[mine, at] = dot(gs, k_s[theirs, at]).astype(BF)
            gk_s[theirs, at] = dot_tn(gs, q_s[mine, at]).astype(BF)
            gv_s[theirs, at] = dot_tn(probs.astype(BF), ga).astype(BF)
        return carry

    for h in range(PARTS):
        total = scatter_end(ga_send.at[h], ga_recv.at[h], ga_in[h])
        ga_s[:, h * part : (h + 1) * part] = total.astype(BF)
        att_in[h].append(forwarded(att.at[h], zz_peer, att_in[h]))
        lax.fori_loop(0, heads, functools.partial(backward, h * heads), 0, unroll=heads)

    for c in range(0, rows_all, tile):
        both = dot_nt(kw[...], gk_s[c : c + tile, :]) + dot_nt(vw[...], gv_s[c : c + tile, :])
        for k in range(tp):
            st_send[k, :, c : c + tile] = both[k * width_part : (k + 1) * width_part].astype(BF)
    st_in = scatter_start(st_send, st_recv, tensor_peer)

    def cross_partial(k):
        slot = flip(apart, k)
        for m in range(g):
            cp_send[k, :, m * cols : (m + 1) * cols] = sum(
                dot(att[h, slot], w[m, h * part : (h + 1) * part, :]) for h in range(PARTS)
            ).astype(BF)

    for copies in att_in:
        copies[0].wait_recv()
        copies[2].wait_recv()
    cross_partial(3)
    cross_partial(1)
    cp_in = scatter_start(cp_send, cp_recv, tensor_peer)
    scatter_middle(st_send, st_recv, tensor_peer, st_in)
    cross_partial(2)
    scatter_middle(cp_send, cp_recv, tensor_peer, cp_in)
    cross_partial(0)

    def hidden_partial(k):
        hp_send[k] = dot_nt(gq_s[...], wq[k]).astype(BF)

    hidden_partial(3)
    hidden_partial(1)
    hp_in = scatter_start(hp_send, hp_recv, tensor_peer)

    rows_s[...] = scatter_end(st_send, st_recv, st_in).astype(BF)
    ret_in = []
    for o in range(1, WINDOW + 1):
        block = sum(
            is_gap(owner_gap[k], o) * rows_s[:, k * pair_rows : (k + 1) * pair_rows].astype(F32)
            for k in range(pairs)
        )
        ret_send[o - 1] = block.astype(BF)
        ret_in.append(send(ret_send.at[o - 1], ret_recv.at[o - 1], dp_peer(o)))

    co_mine[...] = scatter_end(cp_send, cp_recv, cp_in).astype(BF)
    cross_in = remote(co_mine, co_last, turn_peer)

    @pl.when(jnp.logical_not(on_diagonal))
    def _():
        cross_in.start()

    @pl.when(on_diagonal)
    def _():
        co_last[...] = co_mine[...]

    hidden_partial(2)
    scatter_middle(hp_send, hp_recv, tensor_peer, hp_in)
    hidden_partial(0)
    gh_ref[...] = scatter_end(hp_send, hp_recv, hp_in).astype(BF)

    for copy in ret_in:
        copy.wait_recv()
    for k in range(pairs):
        block = sum(
            is_gap(target_gap[k], o) * ret_recv[o - 1].astype(F32) for o in range(1, WINDOW + 1)
        )
        for i in range(CAP):
            gst_ref[k * CAP + i] = block[:, i * block_len : (i + 1) * block_len].astype(BF)

    @pl.when(jnp.logical_not(on_diagonal))
    def _():
        cross_in.wait()

    cross_ref[...] = co_last[...]
    for copy in sent:
        copy.wait_send()


def shards(
    hidden,
    grad_out,
    query_weight,
    key_weight,
    value_weight,
    out_weight,
    neighbour_states,
    block_owner,
    slot_target,
):
    dp_count, tp = lax.axis_size("dp"), lax.axis_size("tensor")
    g = dp_count // tp
    tokens, width = hidden.shape
    local = query_weight.shape[1]
    states = jnp.swapaxes(neighbour_states, 1, 2)
    block_count, width_part, block_len = states.shape
    rows = block_count * block_len
    pair_rows = CAP * block_len
    part = local // PARTS
    heads = HEADS // tp
    copies = 2 * WINDOW + (6 + 2 * PARTS) * (tp - 1) + PARTS * (g - 1) + 2

    def vmem(*shape, kind=BF):
        return pltpu.VMEM(shape, kind)

    in_vmem = pl.BlockSpec(memory_space=pltpu.VMEM)
    anywhere = pl.BlockSpec(memory_space=pl.ANY)
    multiply_adds = tokens * tp * width * local * 4 + rows * local * tp * width_part * 4
    cross, grad_hidden, grad_states = pl.pallas_call(
        functools.partial(kernel, dp_count, tp),
        in_specs=[anywhere] * 9,
        out_specs=[in_vmem] * 3,
        out_shape=[
            jax.ShapeDtypeStruct(hidden.shape, BF),
            jax.ShapeDtypeStruct(hidden.shape, BF),
            jax.ShapeDtypeStruct(states.shape, BF),
        ],
        scratch_shapes=[
            pltpu.SMEM(block_owner.shape, jnp.int32),
            pltpu.SMEM(slot_target.shape, jnp.int32),
            vmem(*states.shape),
            vmem(tp, width, local),
            vmem(tp * width_part, local),
            vmem(tp * width_part, local),
            vmem(g, *out_weight.shape),
            vmem(tp, tokens, width),
            vmem(tp, tokens, width),
            vmem(PARTS, tp, tokens, part),
            vmem(PARTS, tp, tokens, part),
            vmem(WINDOW, width_part, pair_rows),
            vmem(WINDOW, width_part, pair_rows),
            vmem(tp, width_part, rows),
            vmem(rows, tp * width_part),
            vmem(tokens, local),
            vmem(rows, local),
            vmem(rows, local),
            vmem(PARTS, tp, tokens, part),
            vmem(heads, tokens, K_NB * block_len, kind=F32),
            vmem(tokens, local),
            vmem(tokens, local),
            vmem(rows, local),
            vmem(rows, local),
            vmem(tp, width_part, rows),
            vmem(tp, width_part, rows),
            vmem(width_part, rows),
            vmem(WINDOW, width_part, pair_rows),
            vmem(WINDOW, width_part, pair_rows),
            vmem(tp, tokens, width),
            vmem(tp, tokens, width),
            vmem(tp, tokens, width),
            vmem(tp, tokens, width),
            vmem(tokens, width),
            vmem(tokens, width),
            pltpu.SemaphoreType.DMA((copies,)),
            pltpu.SemaphoreType.DMA((copies,)),
            pltpu.SemaphoreType.DMA((3 * tp + 6,)),
        ],
        cost_estimate=pl.CostEstimate(
            flops=2 * multiply_adds, bytes_accessed=16 * 2**20, transcendentals=0
        ),
        compiler_params=pltpu.CompilerParams(
            collective_id=0, has_side_effects=True, vmem_limit_bytes=60 * 2**20
        ),
    )(
        block_owner,
        slot_target,
        hidden,
        grad_out,
        states,
        query_weight,
        key_weight,
        value_weight,
        out_weight,
    )
    return cross, grad_hidden, jnp.swapaxes(grad_states, 1, 2)


def solution(mesh):
    placed = (
        P("dp", "tensor"),
        P("dp", "tensor"),
        P(None, "tensor"),
        P(None, "tensor"),
        P(None, "tensor"),
        P("tensor", "dp"),
        P("dp", None, "tensor"),
        P("dp", None),
        P("dp", None),
    )
    return jax.shard_map(
        shards,
        mesh=mesh,
        in_specs=placed,
        out_specs=(P("dp", "tensor"), P("dp", "tensor"), P("dp", None, "tensor")),
        check_vma=False,
    )
```

```python
import functools
import math

import jax
import jax.numpy as jnp
from jax import lax
from jax.experimental import pallas as pl
from jax.experimental.pallas import tpu as pltpu
from jax.sharding import PartitionSpec as P

HEADS = 32
SPAN = 64
K_NB = 2
CAP = 2
WINDOW = 4
BF = jnp.bfloat16
F32 = jnp.float32


def dot_nt(left, right):
    return lax.dot_general(left, right, (((1,), (1,)), ((), ())), preferred_element_type=F32)


def dot_tn(left, right):
    return lax.dot_general(left, right, (((0,), (0,)), ((), ())), preferred_element_type=F32)


def dot(left, right):
    return jnp.dot(left, right, preferred_element_type=F32)


MESH = pl.DeviceIdType.MESH
PARTS = 2


def flip(i, k):
    if k % 2:
        i = i + 1 - 2 * (i % 2)
    return (i + 2) % 4 if k >= 2 else i


def kernel(
    dp_count,
    tp,
    owner_hbm,
    target_hbm,
    hidden_hbm,
    grad_hbm,
    states_hbm,
    wq_hbm,
    kw_hbm,
    vw_hbm,
    ow_hbm,
    cross_ref,
    gh_ref,
    gst_ref,
    owner_ref,
    target_ref,
    states_ref,
    wq,
    kw,
    vw,
    w,
    hid,
    turned,
    ga_send,
    ga_recv,
    out_blocks,
    arrived,
    nbp,
    nb,
    q_s,
    k_s,
    v_s,
    att,
    probs_s,
    ga_s,
    gq_s,
    gk_s,
    gv_s,
    st_send,
    st_recv,
    rows_s,
    ret_send,
    ret_recv,
    hp_send,
    hp_recv,
    cp_send,
    cp_recv,
    co_mine,
    co_last,
    send_sem,
    recv_sem,
    local_sem,
):
    g = dp_count // tp
    d, t = lax.axis_index("dp"), lax.axis_index("tensor")
    zz, gx = d // g, d % g
    tokens, width = hidden_hbm.shape
    block_count, width_part, block_len = states_ref.shape
    rows_all = block_count * block_len
    pair_rows = CAP * block_len
    pairs = block_count // CAP
    part = q_s.shape[1] // PARTS
    cols = w.shape[2]
    local = q_s.shape[1]
    head_size = local * tp // HEADS
    scale = 1.0 / math.sqrt(head_size)
    spans = tokens // SPAN
    keys = K_NB * block_len

    def tensor_peer(k):
        return (d, flip(t, k))

    def zz_peer(j):
        return (flip(zz, j) * g + gx, t)

    def group_peer(k):
        return (zz * g + (gx + k) % g, t)

    def dp_peer(o):
        return ((d + o + dp_count) % dp_count, t)

    turn_peer = (t * g + gx, zz)
    on_diagonal = t == zz
    apart = (zz + t) % 2 + 2 * ((zz // 2 + t // 2) % 2)

    local_copies = []

    def load(src, dst):
        copy = pltpu.make_async_copy(src, dst, local_sem.at[len(local_copies)])
        copy.start()
        local_copies.append(copy)
        return copy

    load_small = [
        load(owner_hbm, owner_ref),
        load(target_hbm, target_ref),
        load(states_hbm, states_ref),
    ]
    load_hidden = load(hidden_hbm, hid.at[0])
    load_w = load(ow_hbm, w.at[gx])
    load_q, load_kv = [], []
    for k in range(tp):
        load_q.append(load(wq_hbm.at[pl.ds(flip(t, k) * width, width), :], wq.at[k]))
    for k in range(tp):
        for hbm, here in ((kw_hbm, kw), (vw_hbm, vw)):
            rows = pl.ds(flip(t, k) * width_part, width_part)
            load_kv.append(load(hbm.at[rows, :], here.at[pl.ds(k * width_part, width_part), :]))

    barrier = pltpu.get_barrier_semaphore()
    peers = [tensor_peer(1), tensor_peer(2), zz_peer(1), zz_peer(2)]
    peers += [group_peer(k) for k in range(1, g)]
    peers += [dp_peer(o) for o in range(1, WINDOW + 1)]
    peers += [dp_peer(-o) for o in range(1, WINDOW + 1)]
    peers.append(turn_peer)
    for peer in peers:
        pl.semaphore_signal(barrier, inc=1, device_id=peer, device_id_type=MESH)
    pl.semaphore_wait(barrier, len(peers))

    sent = []
    used = [0]

    def remote(src, dst, peer):
        i = used[0]
        used[0] += 1
        return pltpu.make_async_remote_copy(
            src_ref=src,
            dst_ref=dst,
            send_sem=send_sem.at[i],
            recv_sem=recv_sem.at[i],
            device_id=peer,
            device_id_type=MESH,
        )

    def send(src, dst, peer):
        copy = remote(src, dst, peer)
        copy.start()
        sent.append(copy)
        return copy

    def gather(src, slots, peer):
        return [send(src, slots.at[1], peer(1)), send(src, slots.at[2], peer(2))]

    def forwarded(slots, peer, copies):
        copies[1].wait_recv()
        return send(slots.at[2], slots.at[3], peer(1))

    def scatter_start(parts, recv, peer):
        return [send(parts.at[3], recv.at[1], peer(1)), send(parts.at[1], recv.at[0], peer(1))]

    def scatter_middle(parts, recv, peer, copies):
        copies[0].wait_recv()
        parts[2] = (parts[2].astype(F32) + recv[1].astype(F32)).astype(BF)
        copies.append(send(parts.at[2], recv.at[2], peer(2)))

    def scatter_end(parts, recv, copies):
        copies[1].wait_recv()
        copies[2].wait_recv()
        return parts[0].astype(F32) + recv[0].astype(F32) + recv[2].astype(F32)

    def is_gap(gap, o):
        return jnp.where(gap == o, 1.0, 0.0).astype(F32)

    turn_in = remote(grad_hbm, turned.at[0], turn_peer)
    turn_local = pltpu.make_async_copy(grad_hbm, turned.at[0], local_sem.at[len(local_copies)])

    @pl.when(jnp.logical_not(on_diagonal))
    def _():
        turn_in.start()

    @pl.when(on_diagonal)
    def _():
        turn_local.start()

    def send_weight(h):
        rows = pl.ds(h * part, part)
        return [
            send(ow_hbm.at[rows, :], w.at[gx, rows, :], group_peer(k)) for k in range(1, g)
        ]

    weight_in = [send_weight(0)]
    hidden_in = gather(hidden_hbm, hid, tensor_peer)
    weight_in += [send_weight(h) for h in range(1, PARTS)]

    for copy in load_small:
        copy.wait()
    owner_gap = [(owner_ref[0, k * CAP] - d + dp_count) % dp_count for k in range(pairs)]
    target_gap = [(d - target_ref[0, k * CAP] + dp_count) % dp_count for k in range(pairs)]
    blocks_in = []
    for o in range(1, WINDOW + 1):
        for i in range(CAP):
            block = sum(
                is_gap(target_gap[k], o) * states_ref[k * CAP + i].astype(F32)
                for k in range(pairs)
            )
            out_blocks[o - 1, :, i * block_len : (i + 1) * block_len] = block.astype(BF)
        blocks_in.append(send(out_blocks.at[o - 1], arrived.at[o - 1], dp_peer(-o)))

    @pl.when(jnp.logical_not(on_diagonal))
    def _():
        turn_in.wait()

    @pl.when(on_diagonal)
    def _():
        turn_local.wait()

    turned_in = gather(turned.at[0], turned, tensor_peer)

    for copy in blocks_in:
        copy.wait_recv()
    for k in range(pairs):
        block = sum(
            is_gap(owner_gap[k], o) * arrived[o - 1].astype(F32) for o in range(1, WINDOW + 1)
        )
        nbp[0, :, k * pair_rows : (k + 1) * pair_rows] = block.astype(BF)
    nb_in = gather(nbp.at[0], nbp, tensor_peer)

    hidden_in.append(forwarded(hid, tensor_peer, hidden_in))
    turned_in.append(forwarded(turned, tensor_peer, turned_in))
    load_hidden.wait()
    hidden_in[0].wait_recv()
    hidden_in[2].wait_recv()
    for copy in load_q:
        copy.wait()
    tile = min(256, local)
    for c in range(0, local, tile):
        at = pl.ds(c, tile)
        q_s[:, at] = sum(dot(hid[k], wq[k, :, at]) for k in range(tp)).astype(BF)
    nb_in.append(forwarded(nbp, tensor_peer, nb_in))

    load_w.wait()
    turned_in[0].wait_recv()
    turned_in[2].wait_recv()

    def ga_partial(h, j):
        block = turned[flip(apart, j)]
        ga_send[h, j] = sum(
            dot_nt(block[:, m * cols : (m + 1) * cols], w[m, h * part : (h + 1) * part, :])
            for m in range(g)
        ).astype(BF)

    def ga_start(h):
        for copy in weight_in[h]:
            copy.wait_recv()
        ga_partial(h, 3)
        ga_partial(h, 1)
        copies = scatter_start(ga_send.at[h], ga_recv.at[h], zz_peer)
        ga_partial(h, 2)
        ga_partial(h, 0)
        return copies

    ga_in = [ga_start(0)]

    nb_in[0].wait_recv()
    nb_in[2].wait_recv()
    for b in range(block_count):
        block = nbp[:, :, b * block_len : (b + 1) * block_len]
        nb[b * block_len : (b + 1) * block_len, :] = block.reshape(tp * width_part, block_len).T
    for copy in load_kv:
        copy.wait()
    for c in range(0, local, tile):
        at = pl.ds(c, tile)
        k_s[:, at] = dot(nb[...], kw[:, at]).astype(BF)
        v_s[:, at] = dot(nb[...], vw[:, at]).astype(BF)
    scatter_middle(ga_send.at[0], ga_recv.at[0], zz_peer, ga_in[0])
    ga_in += [ga_start(h) for h in range(1, PARTS)]

    heads = local // head_size // PARTS

    def forward(first, n, carry):
        h = first + n
        at = pl.ds(pl.multiple_of(h * head_size, head_size), head_size)
        to = pl.ds(pl.multiple_of(n * head_size, head_size), head_size)
        for c in range(spans):
            mine, theirs = pl.ds(c * SPAN, SPAN), pl.ds(c * keys, keys)
            scores = dot_nt(q_s[mine, at], k_s[theirs, at]) * scale
            expanded = jnp.exp(scores - jnp.max(scores, axis=-1, keepdims=True))
            probs = expanded / jnp.sum(expanded, axis=-1, keepdims=True)
            probs_s[h, mine, :] = probs
            att[first // heads, 0, mine, to] = dot(probs.astype(BF), v_s[theirs, at]).astype(BF)
        return carry

    att_in = []
    for h in range(PARTS):
        lax.fori_loop(0, heads, functools.partial(forward, h * heads), 0, unroll=heads)
        att_in.append(gather(att.at[h, 0], att.at[h], zz_peer))
        if h:
            scatter_middle(ga_send.at[h], ga_recv.at[h], zz_peer, ga_in[h])

    def backward(first, n, carry):
        h = first + n
        at = pl.ds(pl.multiple_of(h * head_size, head_size), head_size)
        for c in range(spans):
            mine, theirs = pl.ds(c * SPAN, SPAN), pl.ds(c * keys, keys)
            probs, ga = probs_s[h, mine, :], ga_s[mine, at]
            gp = dot_nt(ga, v_s[theirs, at])
            gs = (probs * (gp - jnp.sum(probs * gp, axis=-1, keepdims=True)) * scale).astype(BF)
            gq_s[mine, at] = dot(gs, k_s[theirs, at]).astype(BF)
            gk_s[theirs, at] = dot_tn(gs, q_s[mine, at]).astype(BF)
            gv_s[theirs, at] = dot_tn(probs.astype(BF), ga).astype(BF)
        return carry

    for h in range(PARTS):
        total = scatter_end(ga_send.at[h], ga_recv.at[h], ga_in[h])
        ga_s[:, h * part : (h + 1) * part] = total.astype(BF)
        att_in[h].append(forwarded(att.at[h], zz_peer, att_in[h]))
        lax.fori_loop(0, heads, functools.partial(backward, h * heads), 0, unroll=heads)

    for c in range(0, rows_all, tile):
        both = dot_nt(kw[...], gk_s[c : c + tile, :]) + dot_nt(vw[...], gv_s[c : c + tile, :])
        for k in range(tp):
            st_send[k, :, c : c + tile] = both[k * width_part : (k + 1) * width_part].astype(BF)
    st_in = scatter_start(st_send, st_recv, tensor_peer)

    def hidden_partial(k):
        hp_send[k] = dot_nt(gq_s[...], wq[k]).astype(BF)

    hidden_partial(3)
    hidden_partial(1)
    hp_in = scatter_start(hp_send, hp_recv, tensor_peer)
    scatter_middle(st_send, st_recv, tensor_peer, st_in)

    share = g // PARTS

    def cross_partial(c, k):
        slot = flip(apart, k)
        for i in range(share):
            cp_send[c, k, :, i * cols : (i + 1) * cols] = sum(
                dot(att[h, slot], w[c * share + i, h * part : (h + 1) * part, :])
                for h in range(PARTS)
            ).astype(BF)

    def cross_start(c):
        cross_partial(c, 3)
        cross_partial(c, 1)
        copies = scatter_start(cp_send.at[c], cp_recv.at[c], tensor_peer)
        cross_partial(c, 2)
        scatter_middle(cp_send.at[c], cp_recv.at[c], tensor_peer, copies)
        cross_partial(c, 0)
        return copies

    def cross_turn(c):
        co_mine[c] = scatter_end(cp_send.at[c], cp_recv.at[c], cp_in[c]).astype(BF)
        copy = remote(co_mine.at[c], co_last.at[c], turn_peer)

        @pl.when(jnp.logical_not(on_diagonal))
        def _():
            copy.start()

        @pl.when(on_diagonal)
        def _():
            co_last[c] = co_mine[c]

        return copy

    for copies in att_in:
        copies[0].wait_recv()
        copies[2].wait_recv()
    cp_in = [cross_start(0)]

    rows_s[...] = scatter_end(st_send, st_recv, st_in).astype(BF)
    ret_in = []
    for o in range(1, WINDOW + 1):
        block = sum(
            is_gap(owner_gap[k], o) * rows_s[:, k * pair_rows : (k + 1) * pair_rows].astype(F32)
            for k in range(pairs)
        )
        ret_send[o - 1] = block.astype(BF)
        ret_in.append(send(ret_send.at[o - 1], ret_recv.at[o - 1], dp_peer(o)))
    cp_in += [cross_start(c) for c in range(1, PARTS)]
    cross_in = [cross_turn(0)]
    hidden_partial(2)
    scatter_middle(hp_send, hp_recv, tensor_peer, hp_in)
    cross_in += [cross_turn(c) for c in range(1, PARTS)]
    hidden_partial(0)
    gh_ref[...] = scatter_end(hp_send, hp_recv, hp_in).astype(BF)

    for copy in ret_in:
        copy.wait_recv()
    for k in range(pairs):
        block = sum(
            is_gap(target_gap[k], o) * ret_recv[o - 1].astype(F32) for o in range(1, WINDOW + 1)
        )
        for i in range(CAP):
            gst_ref[k * CAP + i] = block[:, i * block_len : (i + 1) * block_len].astype(BF)

    @pl.when(jnp.logical_not(on_diagonal))
    def _():
        for copy in cross_in:
            copy.wait()

    for c in range(PARTS):
        cross_ref[:, c * share * cols : (c + 1) * share * cols] = co_last[c]
    for copy in sent:
        copy.wait_send()


def shards(
    hidden,
    grad_out,
    query_weight,
    key_weight,
    value_weight,
    out_weight,
    neighbour_states,
    block_owner,
    slot_target,
):
    dp_count, tp = lax.axis_size("dp"), lax.axis_size("tensor")
    g = dp_count // tp
    tokens, width = hidden.shape
    local = query_weight.shape[1]
    states = jnp.swapaxes(neighbour_states, 1, 2)
    block_count, width_part, block_len = states.shape
    rows = block_count * block_len
    pair_rows = CAP * block_len
    part = local // PARTS
    heads = HEADS // tp
    copies = 2 * WINDOW + (5 + 3 * PARTS) * (tp - 1) + PARTS * (g - 1) + 1 + PARTS

    def vmem(*shape, kind=BF):
        return pltpu.VMEM(shape, kind)

    in_vmem = pl.BlockSpec(memory_space=pltpu.VMEM)
    anywhere = pl.BlockSpec(memory_space=pl.ANY)
    multiply_adds = tokens * tp * width * local * 4 + rows * local * tp * width_part * 4
    cross, grad_hidden, grad_states = pl.pallas_call(
        functools.partial(kernel, dp_count, tp),
        in_specs=[anywhere] * 9,
        out_specs=[in_vmem] * 3,
        out_shape=[
            jax.ShapeDtypeStruct(hidden.shape, BF),
            jax.ShapeDtypeStruct(hidden.shape, BF),
            jax.ShapeDtypeStruct(states.shape, BF),
        ],
        scratch_shapes=[
            pltpu.SMEM(block_owner.shape, jnp.int32),
            pltpu.SMEM(slot_target.shape, jnp.int32),
            vmem(*states.shape),
            vmem(tp, width, local),
            vmem(tp * width_part, local),
            vmem(tp * width_part, local),
            vmem(g, *out_weight.shape),
            vmem(tp, tokens, width),
            vmem(tp, tokens, width),
            vmem(PARTS, tp, tokens, part),
            vmem(PARTS, tp, tokens, part),
            vmem(WINDOW, width_part, pair_rows),
            vmem(WINDOW, width_part, pair_rows),
            vmem(tp, width_part, rows),
            vmem(rows, tp * width_part),
            vmem(tokens, local),
            vmem(rows, local),
            vmem(rows, local),
            vmem(PARTS, tp, tokens, part),
            vmem(heads, tokens, K_NB * block_len, kind=F32),
            vmem(tokens, local),
            vmem(tokens, local),
            vmem(rows, local),
            vmem(rows, local),
            vmem(tp, width_part, rows),
            vmem(tp, width_part, rows),
            vmem(width_part, rows),
            vmem(WINDOW, width_part, pair_rows),
            vmem(WINDOW, width_part, pair_rows),
            vmem(tp, tokens, width),
            vmem(tp, tokens, width),
            vmem(PARTS, tp, tokens, width // PARTS),
            vmem(PARTS, tp, tokens, width // PARTS),
            vmem(PARTS, tokens, width // PARTS),
            vmem(PARTS, tokens, width // PARTS),
            pltpu.SemaphoreType.DMA((copies,)),
            pltpu.SemaphoreType.DMA((copies,)),
            pltpu.SemaphoreType.DMA((3 * tp + 6,)),
        ],
        cost_estimate=pl.CostEstimate(
            flops=2 * multiply_adds, bytes_accessed=16 * 2**20, transcendentals=0
        ),
        compiler_params=pltpu.CompilerParams(
            collective_id=0, has_side_effects=True, vmem_limit_bytes=58 * 2**20
        ),
    )(
        block_owner,
        slot_target,
        hidden,
        grad_out,
        states,
        query_weight,
        key_weight,
        value_weight,
        out_weight,
    )
    return cross, grad_hidden, jnp.swapaxes(grad_states, 1, 2)


def solution(mesh):
    placed = (
        P("dp", "tensor"),
        P("dp", "tensor"),
        P(None, "tensor"),
        P(None, "tensor"),
        P(None, "tensor"),
        P("tensor", "dp"),
        P("dp", None, "tensor"),
        P("dp", None),
        P("dp", None),
    )
    return jax.shard_map(
        shards,
        mesh=mesh,
        in_specs=placed,
        out_specs=(P("dp", "tensor"), P("dp", "tensor"), P("dp", None, "tensor")),
        check_vma=False,
    )
```
